32 devices in a mesh: groups: 2 (over y), dp: 4 (over z), space: 2 (over x), pair: 2 (over core).
Axes of the slice: x: 2, y: 2, z: 4, core: 2. Of those that a mesh axis runs over, the one named last changes fastest.
Arguments:
- volume: bfloat16 [32, 8, 16, 16, 128], P(('groups', 'dp', 'pair'), 'space'), parts along dimension 0, may hold values from -6 to 6
- tissue: int32 [32, 2048], P(('groups', 'dp', 'pair'), 'space'), parts along dimension 0, may hold values 0 or 1
- brick_count: int32 [16], P(('groups', 'dp', 'pair')), parts along dimension 0, may hold values from 1 to 2, as said below
- first_weight: bfloat16 [3, 3, 3, 128, 128], replicated, may hold values from -0.109375 to 0.109375
- second_weight: bfloat16 [3, 3, 3, 128, 128], replicated, may hold values from -0.109375 to 0.109375
- cotangent: bfloat16 [32, 8, 16, 16, 128], P(('groups', 'dp', 'pair'), 'space'), parts along dimension 0, may hold values from -6 to 6
Outputs:
- input_grad: bfloat16 [32, 8, 16, 16, 128], P(('groups', 'dp', 'pair'), 'space'), parts along dimension 0
- first_weight_grad: float32 [6912, 128], P('groups'), parts along dimension 0
- second_weight_grad: float32 [6912, 128], P('groups'), parts along dimension 0
The draws below stay inside these ranges and needn't reach their ends.
There are 2 independent parts, one for each index of `groups`. The reference program is written for one: setup_inputs(seed, part) draws one part's arguments, and reference() takes and returns one part's arrays. A program takes and returns all parts, laid end to end along the dimension named above; an argument that names none is the same for every part. Nothing has to cross between parts.
Inputs may be any that keep to these rules, and one draw needn't show every extreme that they name: `brick_count`: the number of active bricks of an owner; they are its first slots, the other slots are unused.
All inputs are finite; a program needn't handle non-finite values. No bound on the sum of `tissue` on one device may be relied on, other than what follows from the above.
Results may differ from the reference program's by a relative error of at most 0.0059.
Values may be sent and summed in bfloat16 or wider, within the bound.
A program may use at most 64 MiB of HBM per device.

```python
import jax
import jax.numpy as jnp
from jax import lax

C = 128
SLOTS = 2
SLAB = 4
EDGE = 16
BRICK_OWNERS = 8
BRICKS = 16
BRICK_Z = 8


def draw_brick_count(key, part):
    key = jax.random.fold_in(key, 7)
    key_levels, key_chosen = jax.random.split(key)
    levels = jax.random.randint(key_levels, (BRICK_OWNERS,), 0, 8)
    lowest = max(1, SLOTS // 10)
    counts = lowest + (SLOTS - lowest) * levels * levels * levels // 343
    chosen = jax.random.permutation(key_chosen, BRICK_OWNERS)
    owners = jnp.arange(BRICK_OWNERS)
    counts = jnp.where(owners == chosen[1], lowest, counts)
    counts = jnp.where(owners == chosen[0], SLOTS, counts)
    return counts.astype(jnp.int32)


def place_ends(result, rng, low, largest):
    longest = result.shape.index(max(result.shape))
    spots = []
    for shift in (0, 1):
        where = [jax.random.randint(jax.random.fold_in(rng, axis), (), 0, length) for axis, length in enumerate(result.shape)]
        where[longest] = (where[longest] + shift) % result.shape[longest]
        spots.append(tuple(where))
    return result.at[spots[0]].set(low).at[spots[1]].set(largest)


def steps_of(own_key, dims, cuts, low, high):
    def one(position, shards_of):
        heights = jax.random.uniform(jax.random.fold_in(jax.random.fold_in(own_key, 6), position), (shards_of,), jnp.float32, low / len(cuts), high / len(cuts))
        return jnp.repeat(jnp.exp(heights), dims[position] // shards_of).reshape((-1,) + (1,) * (len(dims) - position - 1))

    gain = one(*cuts[0])
    for cut in cuts[1:]:
        gain = gain * one(*cut)
    return gain


def scatter_about(key, extent, scale, most, cuts=(), kind=jnp.bfloat16):
    entries = jax.random.normal(key, extent, jnp.float32) * scale
    if len(cuts) > 0:
        entries = steps_of(key, extent, cuts, -0.22, 0.18) * entries
    return jnp.clip(entries, min=-most, max=most).astype(kind)


def setup_inputs(seed: int = 0, part: int = 0) -> dict:
    streams_of = jax.random.split(jax.random.key(seed), 7)
    own_keys = jax.random.split(jax.random.fold_in(streams_of[6], part), 7)
    volume = scatter_about(own_keys[0], (BRICKS, BRICK_Z, EDGE, EDGE, C), 1.0, 6.0, ((0, 8), (1, 2)))
    tissue = place_ends((jax.random.randint(own_keys[1], (BRICKS, BRICK_Z * EDGE * EDGE), 0, 4) < 3).astype(jnp.int32), jax.random.fold_in(own_keys[1], 1), 0, 1)
    brick_count = draw_brick_count(jax.random.fold_in(jax.random.fold_in(streams_of[6], part), 71), part)
    first_weight = scatter_about(streams_of[3], (3, 3, 3, C, C), (27 * C) ** -0.5, 0.109375)
    second_weight = scatter_about(streams_of[4], (3, 3, 3, C, C), (27 * C) ** -0.5, 0.109375)
    cotangent = scatter_about(own_keys[5], (BRICKS, BRICK_Z, EDGE, EDGE, C), 1.0, 6.0, ((0, 8), (1, 2)))
    return dict(volume=volume, tissue=tissue, brick_count=brick_count, first_weight=first_weight, second_weight=second_weight, cotangent=cotangent)


def unfold_brick(field_in):
    depth_cells = field_in.shape[0]
    edge_cells = field_in.shape[1]
    framed = jnp.pad(field_in, ((1, 1), (1, 1), (1, 1), (0, 0)))
    pieces = []
    for shift_z in range(3):
        for shift_y in range(3):
            for shift_x in range(3):
                pieces.append(framed[shift_z:shift_z + depth_cells, shift_y:shift_y + edge_cells, shift_x:shift_x + edge_cells, :])
    joined = jnp.concatenate(pieces, axis=-1)
    return joined.reshape(depth_cells * edge_cells * edge_cells, joined.shape[-1])


def slope(pre_act):
    sigmoid_of = jax.nn.sigmoid(pre_act)
    return sigmoid_of * (1.0 + pre_act * (1.0 - sigmoid_of))


def reference(volume, tissue, brick_count, first_weight, second_weight, cotangent):
    channels = volume.shape[-1]
    shape_one = volume.shape[1:]
    first_flat = first_weight.reshape(27 * channels, channels)
    second_flat = second_weight.reshape(27 * channels, channels)
    first_back = jnp.swapaxes(jnp.flip(first_weight, (0, 1, 2)), 3, 4).reshape(27 * channels, channels)
    second_back = jnp.swapaxes(jnp.flip(second_weight, (0, 1, 2)), 3, 4).reshape(27 * channels, channels)
    brick_ids = jnp.arange(BRICKS, dtype=jnp.int32)
    active = (brick_ids % SLOTS < brick_count[brick_ids // SLOTS]).astype(jnp.float32)
    gates = tissue.reshape(BRICKS, BRICK_Z, EDGE, EDGE, 1).astype(jnp.float32) * active[:, None, None, None, None]
    contract = (((0,), (0,)), ((), ()))

    def one_brick(state_now, items):
        grad_first, grad_second = state_now
        vol_brick, cot_brick, gating = items
        columns = unfold_brick(vol_brick)
        pre_one = jnp.dot(columns, first_flat, preferred_element_type=jnp.float32).reshape(shape_one)
        hidden = (jax.nn.silu(pre_one) * gating).astype(jnp.bfloat16)
        hidden_cols = unfold_brick(hidden)
        pre_two = jnp.dot(hidden_cols, second_flat, preferred_element_type=jnp.float32).reshape(shape_one)
        error_two = (cot_brick.astype(jnp.float32) * gating * slope(pre_two)).astype(jnp.bfloat16)
        grad_second = grad_second + lax.dot_general(hidden_cols, error_two.reshape(-1, channels), contract, preferred_element_type=jnp.float32)
        back_one = jnp.dot(unfold_brick(error_two), second_back, preferred_element_type=jnp.float32).reshape(shape_one)
        error_one = (back_one * gating * slope(pre_one)).astype(jnp.bfloat16)
        grad_first = grad_first + lax.dot_general(columns, error_one.reshape(-1, channels), contract, preferred_element_type=jnp.float32)
        input_back = jnp.dot(unfold_brick(error_one), first_back, preferred_element_type=jnp.float32).reshape(shape_one)
        return (grad_first, grad_second), input_back.astype(jnp.bfloat16)

    zero_grad = jnp.zeros((27 * channels, channels), jnp.float32)
    totals, input_grad = lax.scan(one_brick, (zero_grad, zero_grad), (volume, cotangent, gates))
    scale_factor = (SLOTS * SLAB * EDGE * EDGE) ** -0.5
    return input_grad, totals[0] * scale_factor, totals[1] * scale_factor
```

```python
import functools

import jax
import jax.numpy as jnp
from jax import lax
from jax.experimental import pallas as pl
from jax.experimental.pallas import tpu as pltpu
from jax.sharding import PartitionSpec as P

BF = jnp.bfloat16
F32 = jnp.float32
MESH = pl.DeviceIdType.MESH


def remote(src, dst, send_sem, recv_sem, where):
    return pltpu.make_async_remote_copy(
        src_ref=src, dst_ref=dst, send_sem=send_sem, recv_sem=recv_sem,
        device_id=where, device_id_type=MESH,
    )


def kernel(D, S, N2, vol, cot, gate, w1, w2, out, g1, g2,
           fv, fh, fe2, fe1, k1, k2, k2b, k1b, sg1, e1t, e2t, grad,
           edges, halo, ps, pr, xs, xr, zs, zr,
           hs_sem, hr_sem, p_s, p_r, x_s, x_r, z_s, z_r, za_s, za_r, xa_s, xa_r, pa_s, pa_r):
    B, Z, M, C = vol.shape
    E = fv.shape[3]
    d, x, c = lax.axis_index("dp"), lax.axis_index("space"), lax.axis_index("pair")
    RC = N2
    R2 = RC // S
    R3 = R2 // D

    barrier = pltpu.get_barrier_semaphore()
    pl.semaphore_signal(barrier, inc=1, device_id={"pair": 1 - c}, device_id_type=MESH)
    for k in range(1, S):
        pl.semaphore_signal(barrier, inc=1, device_id={"space": lax.rem(x + k, S)}, device_id_type=MESH)
    for k in range(1, D):
        pl.semaphore_signal(barrier, inc=1, device_id={"dp": lax.rem(d + k, D)}, device_id_type=MESH)
    pl.semaphore_wait(barrier, 1 + (S - 1) + (D - 1))

    def halo_copies(f, b):
        if f == 0:
            top, bottom = vol.at[b, Z - 1], vol.at[b, 0]
        else:
            top, bottom = edges.at[f - 1, b, 1], edges.at[f - 1, b, 0]
        up = remote(top, halo.at[f, b, 0], hs_sem.at[f, b, 0], hr_sem.at[f, b, 0],
                    {"space": jnp.minimum(x + 1, S - 1)})
        down = remote(bottom, halo.at[f, b, 1], hs_sem.at[f, b, 1], hr_sem.at[f, b, 1],
                      {"space": jnp.maximum(x - 1, 0)})
        return up, down

    def halo_start(f, b):
        up, down = halo_copies(f, b)

        @pl.when(x < S - 1)
        def _():
            up.start()

        @pl.when(x > 0)
        def _():
            down.start()

    row = lax.rem(lax.broadcasted_iota(jnp.int32, (M, C), 0), E)

    def put(field, b, z, val):
        low = jnp.where(row == 0, 0.0, pltpu.roll(val, 1, 0)).astype(BF)
        high = jnp.where(row == E - 1, 0.0, pltpu.roll(val, M - 1, 0)).astype(BF)
        field[b, z, 1 : E + 1] = jnp.concatenate([low, val.astype(BF), high], axis=-1).reshape(E, E, 3 * C)

    def halo_finish(f, field, b):
        up, down = halo_copies(f, b)

        @pl.when(x < S - 1)
        def _():
            up.wait_send()
            down.wait_recv()
            put(field, b, Z + 1, halo[f, b, 1].astype(F32))

        @pl.when(x > 0)
        def _():
            down.wait_send()
            up.wait_recv()
            put(field, b, 0, halo[f, b, 0].astype(F32))

    for b in range(B):
        halo_start(0, b)

    for field in (fv, fh, fe2, fe1):
        for b in range(B):
            zero_row = jnp.zeros((Z + 2, E, 3 * C), BF)
            field[b, :, 0] = zero_row
            field[b, :, E + 1] = zero_row

            @pl.when(x == 0)
            def _():
                field[b, 0] = jnp.zeros((E + 2, E, 3 * C), BF)

            @pl.when(x == S - 1)
            def _():
                field[b, Z + 1] = jnp.zeros((E + 2, E, 3 * C), BF)

    for wide in (k1, k2, k2b, k1b):
        wide[27 * C :, :C] = jnp.zeros((9 * C, C), BF)
        wide[: 9 * C, C:] = jnp.zeros((9 * C, C), BF)

    def build(o, carry):
        at = pl.ds(pl.multiple_of(o * C, C), C)
        later = pl.ds(pl.multiple_of((o + 9) * C, C), C)
        back = pl.ds(pl.multiple_of((26 - o) * C, C), C)
        back_later = pl.ds(pl.multiple_of((35 - o) * C, C), C)
        for src, wide, wide_back in ((w1, k1, k1b), (w2, k2, k2b)):
            block = src[at, :]
            wide[at, :C] = block
            wide[later, C:] = block
            turned = block.T
            wide_back[back, :C] = turned
            wide_back[back_later, C:] = turned
        return carry

    lax.fori_loop(0, 27, build, 0)

    def fill(i, carry):
        b, z = i // Z, lax.rem(i, Z)
        put(fv, b, z + 1, vol[b, z].astype(F32))
        return carry

    lax.fori_loop(0, B * Z, fill, 0)

    def conv(field, b, zp, wide):
        parts = []
        for l in range(4):
            for dy in range(3):
                parts.append(field[b, 2 * zp + l, dy : dy + E].reshape(M, 3 * C))
        got = jnp.dot(jnp.concatenate(parts, axis=-1), wide[...], preferred_element_type=F32)
        return got[:, :C], got[:, C:]

    def phase(f, b, field, wide, use):
        halo_finish(f, field, b)

        def body(zp, carry):
            for t, val in enumerate(conv(field, b, zp, wide)):
                use(b, 2 * zp + t, val)
            return carry

        lax.fori_loop(0, Z // 2, body, 0)

    def after(f, b, field):
        edges[f - 1, b, 0] = field[b, 1, 1 : E + 1].reshape(M, 3 * C)[:, C : 2 * C]
        edges[f - 1, b, 1] = field[b, Z, 1 : E + 1].reshape(M, 3 * C)[:, C : 2 * C]
        halo_start(f, b)

    def use_one(b, z, pre):
        s = jax.nn.sigmoid(pre)
        gating = gate[b, z].astype(F32)
        sg1[b, z] = gating * (s * (1.0 + pre * (1.0 - s)))
        put(fh, b, z + 1, pre * s * gating)

    def lanes(b, z):
        return pl.ds(pl.multiple_of((b * Z + z) * M, M), M)

    def use_two(b, z, pre):
        s = jax.nn.sigmoid(pre)
        val = cot[b, z].astype(F32) * gate[b, z].astype(F32) * (s * (1.0 + pre * (1.0 - s)))
        put(fe2, b, z + 1, val)
        e2t[:, lanes(b, z)] = val.T.astype(BF)

    def use_three(b, z, back):
        val = back * sg1[b, z]
        put(fe1, b, z + 1, val)
        e1t[:, lanes(b, z)] = val.T.astype(BF)

    def use_four(b, z, back):
        out[b, z] = back.astype(BF)

    def gradient(g, field, turned):
        def body(i, carry):
            dz, dy = i // 3, lax.rem(i, 3)
            total = None
            for b in range(B):
                cols = field[b, pl.ds(dz, Z), pl.ds(dy, E)].reshape(Z * M, 3 * C)
                term = jnp.dot(turned[:, b * Z * M : (b + 1) * Z * M], cols, preferred_element_type=F32)
                total = term if total is None else total + term
            for dx in range(3):
                grad[g, pl.ds(pl.multiple_of((i * 3 + dx) * C, C), C), :] = total[:, dx * C : (dx + 1) * C]
            return carry

        lax.fori_loop(0, 9, body, 0)

    outs = (g1, g2)

    def pair_copy(g):
        return remote(ps.at[g], pr.at[g], p_s.at[g], p_r.at[g], {"pair": 1 - c})

    def pair_start(g):
        ps[g] = grad[g, pl.ds(pl.multiple_of((1 - c) * RC, 16), RC), :].astype(BF)
        pair_copy(g).start()

    def space_copy(g, k):
        to = lax.rem(x + k, S)
        return remote(xs.at[g, to], xr.at[g, k - 1], x_s.at[g, k - 1], x_r.at[g, k - 1], {"space": to})

    def mine(g):
        return grad.at[g, pl.ds(pl.multiple_of(c * RC, 16), RC), :]

    def space_start(g):
        pair_copy(g).wait()
        total = mine(g)[...] + pr[g].astype(F32)
        mine(g)[...] = total
        xs[g] = total.astype(BF).reshape(S, R2, C)
        for k in range(1, S):
            space_copy(g, k).start()

    def dp_copy(g, k):
        to = lax.rem(d + k, D)
        return remote(zs.at[g, to], zr.at[g, k - 1], z_s.at[g, k - 1], z_r.at[g, k - 1], {"dp": to})

    def mid(g):
        return grad.at[g, pl.ds(pl.multiple_of(c * RC + x * R2, 16), R2), :]

    def dp_start(g):
        total = mid(g)[...]
        for k in range(1, S):
            space_copy(g, k).wait()
            total = total + xr[g, k - 1].astype(F32)
        mid(g)[...] = total
        zs[g] = total.astype(BF).reshape(D, R3, C)
        for k in range(1, D):
            dp_copy(g, k).start()

    def dp_gather(g, k, owner):
        spot = outs[g].at[c, x, owner]
        return remote(spot, spot, za_s.at[g, k - 1], za_r.at[g, k - 1], {"dp": lax.rem(d + k, D)})

    def gather_start(g):
        total = grad[g, pl.ds(pl.multiple_of(c * RC + x * R2 + d * R3, 16), R3), :]
        for k in range(1, D):
            dp_copy(g, k).wait()
            total = total + zr[g, k - 1].astype(F32)
        outs[g][c, x, d] = total.astype(BF)
        for k in range(1, D):
            dp_gather(g, k, d).start()

    def space_gather(g, k, owner):
        spot = outs[g].at[c, owner]
        return remote(spot, spot, xa_s.at[g, k - 1], xa_r.at[g, k - 1], {"space": lax.rem(x + k, S)})

    def space_gather_start(g):
        for k in range(1, D):
            dp_gather(g, k, d).wait_send()
            dp_gather(g, k, lax.rem(d - k + D, D)).wait_recv()
        for k in range(1, S):
            space_gather(g, k, x).start()

    def pair_gather(g, owner):
        spot = outs[g].at[owner]
        return remote(spot, spot, pa_s.at[g], pa_r.at[g], {"pair": 1 - c})

    def pair_gather_start(g):
        for k in range(1, S):
            space_gather(g, k, x).wait_send()
            space_gather(g, k, lax.rem(x - k + S, S)).wait_recv()
        pair_gather(g, c).start()

    def finish(g):
        pair_gather(g, c).wait_send()
        pair_gather(g, 1 - c).wait_recv()

    pad = 2 * RC - 27 * C
    if pad:
        for g in range(2):
            grad[g, 27 * C :, :] = jnp.zeros((pad, C), F32)

    for b in range(B):
        phase(0, b, fv, k1, use_one)
        after(1, b, fh)
    for b in range(B):
        phase(1, b, fh, k2, use_two)
        after(2, b, fe2)
    gradient(1, fh, e2t)
    pair_start(1)
    for b in range(B):
        phase(2, b, fe2, k2b, use_three)
        after(3, b, fe1)
        if b == 0:
            space_start(1)
    dp_start(1)
    gradient(0, fv, e1t)
    pair_start(0)
    gather_start(1)
    phase(3, 0, fe1, k1b, use_four)
    space_start(0)
    space_gather_start(1)
    for b in range(1, B):
        phase(3, b, fe1, k1b, use_four)
    dp_start(0)
    pair_gather_start(1)
    gather_start(0)
    space_gather_start(0)
    pair_gather_start(0)
    finish(1)
    finish(0)


def local(D, S, volume, tissue, brick_count, first_weight, second_weight, cotangent):
    B, Z, E, _, C = volume.shape
    M = E * E
    active = (jnp.arange(B, dtype=jnp.int32) < brick_count[0]).astype(jnp.int32)
    gate = jnp.broadcast_to((tissue * active[:, None]).astype(BF).reshape(B, Z, M, 1), (B, Z, M, C))
    unit = 16 * D * S
    RC = -(-27 * C // (2 * unit)) * unit
    R3 = RC // (D * S)
    field = pltpu.VMEM((B, Z + 2, E + 2, E, 3 * C), BF)
    wide = pltpu.VMEM((36 * C, 2 * C), BF)
    dma = pltpu.SemaphoreType.DMA
    s1, d1 = max(S - 1, 1), max(D - 1, 1)
    in_grad, g1, g2 = pl.pallas_call(
        functools.partial(kernel, D, S, RC),
        out_shape=(
            jax.ShapeDtypeStruct((B, Z, M, C), BF),
            jax.ShapeDtypeStruct((2, S, D, R3, C), BF),
            jax.ShapeDtypeStruct((2, S, D, R3, C), BF),
        ),
        in_specs=[pl.BlockSpec(memory_space=pltpu.VMEM)] * 5,
        out_specs=tuple([pl.BlockSpec(memory_space=pltpu.VMEM)] * 3),
        scratch_shapes=[
            field, field, field, field, wide, wide, wide, wide,
            pltpu.VMEM((B, Z, M, C), F32),
            pltpu.VMEM((C, B * Z * M), BF),
            pltpu.VMEM((C, B * Z * M), BF),
            pltpu.VMEM((2, 2 * RC, C), F32),
            pltpu.VMEM((3, B, 2, M, C), BF),
            pltpu.VMEM((4, B, 2, M, C), BF),
            pltpu.VMEM((2, RC, C), BF),
            pltpu.VMEM((2, RC, C), BF),
            pltpu.VMEM((2, S, RC // S, C), BF),
            pltpu.VMEM((2, s1, RC // S, C), BF),
            pltpu.VMEM((2, D, R3, C), BF),
            pltpu.VMEM((2, d1, R3, C), BF),
            dma((4, B, 2)), dma((4, B, 2)),
            dma((2,)), dma((2,)),
            dma((2, s1)), dma((2, s1)),
            dma((2, d1)), dma((2, d1)),
            dma((2, d1)), dma((2, d1)),
            dma((2, s1)), dma((2, s1)),
            dma((2,)), dma((2,)),
        ],
        compiler_params=pltpu.CompilerParams(
            collective_id=0, has_side_effects=True, vmem_limit_bytes=56 * 1024 * 1024
        ),
    )(
        volume.reshape(B, Z, M, C),
        cotangent.reshape(B, Z, M, C),
        gate,
        first_weight.reshape(27 * C, C),
        second_weight.reshape(27 * C, C),
    )
    scale = 2048 ** -0.5

    def finished(g):
        blocks = g.reshape(2 * RC, C)[: 27 * C].reshape(27, C, C)
        return (jnp.swapaxes(blocks, 1, 2).astype(F32) * scale).reshape(27 * C, C)

    return in_grad.reshape(volume.shape), finished(g1), finished(g2)


def solution(mesh):
    bricks = P(("groups", "dp", "pair"), "space", None, None, None)
    in_specs = (
        bricks,
        P(("groups", "dp", "pair"), "space"),
        P(("groups", "dp", "pair")),
        P(),
        P(),
        bricks,
    )
    out_specs = (bricks, P("groups", None), P("groups", None))
    run = functools.partial(local, mesh.shape["dp"], mesh.shape["space"])
    return jax.shard_map(run, mesh=mesh, in_specs=in_specs, out_specs=out_specs, check_vma=False)
```
